32 devices in a mesh: row: 4 (over y, x), col: 8 (over z, core).
Axes of the slice: x: 2, y: 2, z: 4, core: 2. Of those that a mesh axis runs over, the one named last changes fastest.
Arguments:
- tensor: float32 [2048, 8192], P('row', 'col'), may hold values from -60 to 60, as said below
- factor: float32 [2048, 256], P('row'), may hold values from -0.125 to 0.125
Outputs:
- gram: float32 [2048, 2048], P('col', 'row')
- core: float32 [256, 8192], P('row', 'col')
The draws below stay inside these ranges and needn't reach their ends.
Inputs may be any that keep to these rules, and one draw needn't show every extreme that they name: `tensor`: values of the unfolded field.
All inputs are finite; a program needn't handle non-finite values.
Results may differ from the reference program's by a relative error of at most 0.000096.
Values sent between devices are 32-bit elements; how exact they have to be, the bound alone decides.
No kernel may reach another device: no remote copies, remote signals or barrier semaphores. Data moves between devices by JAX's collectives and lax.ppermute only.
A program may use at most 64 MiB of HBM per device.

```python
import math
import jax
import jax.numpy as jnp
from jax import lax

I1 = 2048
RANK = 256
NCOLS = 8192


def draw_tensor(key, part):
    key = jax.random.fold_in(key, 11)
    key_base, key_rows, key_cols = jax.random.split(key, 3)
    row_scale = jnp.exp(jax.random.uniform(key_rows, (I1, 1), jnp.float32, math.log(0.3), math.log(3.0)))
    col_scale = jnp.exp(jax.random.uniform(key_cols, (1, NCOLS), jnp.float32, math.log(0.3), math.log(3.0)))
    values = jax.random.normal(key_base, (I1, NCOLS), jnp.float32) * row_scale * col_scale
    return jnp.clip(values, -60.0, 60.0)


def block_levels(key, shape, cuts, least, largest):
    loudness, own = 1.0, jax.random.fold_in(key, 6)
    for dim, blocks in cuts:
        draws = jnp.exp(jax.random.uniform(jax.random.fold_in(own, dim), (blocks,), jnp.float32, least / len(cuts), largest / len(cuts)))
        loudness = loudness * jnp.repeat(draws, shape[dim] // blocks).reshape([-1 if axis == dim else 1 for axis in range(len(shape))])
    return loudness


def noise(stream_key, dims, spread, limit, cuts=(), kind=jnp.bfloat16):
    values = spread * jax.random.normal(stream_key, dims, jnp.float32)
    if cuts:
        values = values * block_levels(stream_key, dims, cuts, -0.22, 0.18)
    return jnp.clip(values, -limit, limit).astype(kind)


def setup_inputs(seed: int = 0) -> dict:
    arg_keys = jax.random.split(jax.random.key(seed), 3)
    tensor = draw_tensor(jax.random.fold_in(arg_keys[2], 71), 0)
    factor = noise(arg_keys[1], (I1, RANK), I1 ** -0.5, 0.125, ((0, 4),), jnp.float32)
    return {"tensor": tensor, "factor": factor}


def reference(tensor, factor):
    highest = lax.Precision.HIGHEST
    gram = jnp.dot(tensor, tensor.T, precision=highest, preferred_element_type=jnp.float32) / NCOLS
    core = jnp.dot(factor.T, tensor, precision=highest, preferred_element_type=jnp.float32)
    return gram, core
```

```python
import jax
import jax.numpy as jnp
import numpy as np
from jax import lax
from jax.sharding import PartitionSpec as P

AXES = ("row", "col")
CORES = 2


def contract_last(left, right):
    return lax.dot_general(
        left,
        right,
        (((1,), (1,)), ((), ())),
        precision=lax.Precision.HIGHEST,
        preferred_element_type=jnp.float32,
    )


def multiply(left, right):
    return lax.dot_general(
        left,
        right,
        (((1,), (0,)), ((), ())),
        precision=lax.Precision.HIGHEST,
        preferred_element_type=jnp.float32,
    )


class Layout:
    def __init__(self, rows, cols):
        self.rows, self.cols, self.chips = rows, cols, cols // CORES
        assert rows % 2 == 0 and cols % CORES == 0 and self.chips % rows == 0
        self.subs = self.chips // rows
        self.ring = [*range(0, rows, 2), *reversed(range(1, rows, 2))]
        self.place = {r: i for i, r in enumerate(self.ring)}
        self.devices = [(r, z, c) for r in range(rows) for z in range(self.chips) for c in range(CORES)]

    def flat(self, r, z, c):
        return r * self.cols + z * CORES + c

    def along(self, r, c, steps):
        return self.ring[(self.place[r] + (steps if c == 0 else -steps)) % self.rows]

    def swap(self):
        return [(self.flat(r, z, c), self.flat(r, z, 1 - c)) for r, z, c in self.devices]

    def fetch(self, steps):
        return [(self.flat(self.along(r, c, steps), z, c), self.flat(r, z, c)) for r, z, c in self.devices]

    def keeper(self, first, size, target):
        last = min(first + size, self.chips) - 1
        return min(max(target, first), last)

    def sums(self, steps, sub):
        rounds = []
        size = 1
        while size < self.chips:
            pairs = []
            for r in range(self.rows):
                for c in range(CORES):
                    target = self.along(r, c, steps) * self.subs + sub
                    for first in range(0, self.chips, 2 * size):
                        if first + size >= self.chips:
                            continue
                        a = self.keeper(first, size, target)
                        b = self.keeper(first + size, size, target)
                        to = self.keeper(first, 2 * size, target)
                        pairs.append((self.flat(r, a + b - to, c), self.flat(r, to, c)))
            rounds.append(pairs)
            size *= 2
        return rounds

    def classes(self):
        table = np.zeros((self.rows, self.cols), np.int32)
        for r, z, c in self.devices:
            ahead = self.place[z // self.subs] - self.place[r]
            table[r, z * CORES + c] = (ahead if c == 0 else -ahead) % self.rows
        return table


def body(tensor, factor):
    layout = Layout(lax.axis_size("row"), lax.axis_size("col"))
    rows, subs = layout.rows, layout.subs
    block, width = tensor.shape
    inverse = 1.0 / (width * layout.cols)
    row, col = lax.axis_index("row"), lax.axis_index("col")
    core = lax.rem(col, CORES)
    part = block // (subs * CORES)
    half = subs * part

    def send(value, pairs):
        return lax.ppermute(value, AXES, pairs)

    def my_rows(value):
        split = value.reshape(subs, CORES, part, value.shape[1])
        return lax.dynamic_index_in_dim(split, core, 1, keepdims=False).reshape(half, value.shape[1])

    def add_up(value, steps, sub):
        for pairs in layout.sums(steps, sub):
            value = value + send(value, pairs)
        return value

    near = my_rows(tensor)
    other = send(tensor, layout.swap())
    far = my_rows(other)

    def grams(near_rows, far_rows):
        return contract_last(near_rows, tensor) + contract_last(far_rows, other)

    forward, backward = rows // 2, (rows - 1) // 2
    blocks = {0: (near, far)}
    last = forward
    for steps in range(1, forward):
        before = blocks[steps - 1]
        blocks[steps] = tuple(send(b, layout.fetch(1)) for b in before)
    for steps in range(1, backward + 1):
        before = blocks[(rows - steps + 1) % rows]
        blocks[rows - steps] = tuple(send(b, layout.fetch(-1)) for b in before)

    both = jnp.concatenate(blocks[last - 1], axis=1).reshape(subs, part, 2 * width)
    cuts = [0, part // 2, part * 3 // 4, part]
    pieces = [
        send(both[:, a:b].reshape(subs * (b - a), 2 * width), layout.fetch(1)) for a, b in zip(cuts, cuts[1:])
    ]

    summed = {}
    for steps, (n, f) in blocks.items():
        product = grams(n, f).reshape(subs, part, block)
        summed[steps] = [add_up(product[s], steps, s) for s in range(subs)]
    tail = []
    for piece in pieces:
        product = grams(piece[:, :width], piece[:, width:]).reshape(subs, -1, block)
        tail.append([add_up(product[s], last, s) for s in range(subs)])
    summed[last] = [jnp.concatenate([t[s] for t in tail], axis=0) for s in range(subs)]

    kind = jnp.asarray(layout.classes())[row, col]
    sub = lax.rem(col // CORES, subs)
    gram = jnp.zeros((part, block), jnp.float32)
    for steps, values in summed.items():
        for s, value in enumerate(values):
            gram = jnp.where((kind == steps) & (sub == s), value, gram)
    gram = gram * inverse

    rank = factor.shape[1] // rows
    columns = my_rows(factor).T.reshape(rows, rank, half)
    ring = jnp.asarray(np.array([[[layout.along(r, c, s) for s in range(rows)] for c in range(CORES)] for r in range(rows)]))
    total = None
    for steps in range(rows):
        mine = lax.dynamic_index_in_dim(columns, ring[row, core, (rows - steps) % rows], 0, keepdims=False)
        weights = send(mine, layout.fetch(steps)) if steps else mine
        if steps == last:
            share = 0.0
            weights = weights.reshape(rank, subs, part)
            for (a, b), piece in zip(zip(cuts, cuts[1:]), pieces):
                share = share + multiply(weights[:, :, a:b].reshape(rank, -1), piece)
            near_share, far_share = share[:, :width], share[:, width:]
        else:
            near_share, far_share = (multiply(weights, b) for b in blocks[steps])
        total = (near_share, far_share) if total is None else (total[0] + near_share, total[1] + far_share)
    core_rows = total[0] + send(total[1], layout.swap())
    return (gram, core_rows)


def solution(mesh):
    placed = (P("row", "col"), P("row", None))
    return jax.shard_map(
        body,
        mesh=mesh,
        in_specs=placed,
        out_specs=(P("col", "row"), P("row", "col")),
        check_vma=False,
    )
```

```python
import functools

import jax
import jax.numpy as jnp
import numpy as np
from jax import lax
from jax.experimental import pallas as pl
from jax.experimental.pallas import tpu as pltpu
from jax.sharding import PartitionSpec as P

AXES = ("row", "col")
CORES = 2
FLOPS = 1_200_000_000
PARAMS = pltpu.CompilerParams(vmem_limit_bytes=40 * 2**20)


def shape(*dims, dtype=jnp.float32):
    return jax.ShapeDtypeStruct(dims, dtype)


class Layout:
    def __init__(self, rows, cols):
        self.rows, self.cols, self.chips = rows, cols, cols // CORES
        assert rows % 2 == 0 and cols % CORES == 0 and self.chips % rows == 0
        self.subs = self.chips // rows
        self.ring = [*range(0, rows, 2), *reversed(range(1, rows, 2))]
        self.place = {r: i for i, r in enumerate(self.ring)}
        self.devices = [(r, z, c) for r in range(rows) for z in range(self.chips) for c in range(CORES)]

    def flat(self, r, z, c):
        return r * self.cols + z * CORES + c

    def along(self, r, c, steps):
        return self.ring[(self.place[r] + (steps if c == 0 else -steps)) % self.rows]

    def swap(self):
        return [(self.flat(r, z, c), self.flat(r, z, 1 - c)) for r, z, c in self.devices]

    def fetch(self, steps):
        return [(self.flat(self.along(r, c, steps), z, c), self.flat(r, z, c)) for r, z, c in self.devices]

    def keeper(self, first, size, target):
        last = min(first + size, self.chips) - 1
        return min(max(target, first), last)

    def sums(self, steps, sub):
        rounds = []
        size = 1
        while size < self.chips:
            pairs = []
            for r in range(self.rows):
                for c in range(CORES):
                    target = self.along(r, c, steps) * self.subs + sub
                    for first in range(0, self.chips, 2 * size):
                        if first + size >= self.chips:
                            continue
                        a = self.keeper(first, size, target)
                        b = self.keeper(first + size, size, target)
                        to = self.keeper(first, 2 * size, target)
                        pairs.append((self.flat(r, a + b - to, c), self.flat(r, to, c)))
            rounds.append(pairs)
            size *= 2
        return rounds

    def classes(self):
        table = np.zeros((self.rows, self.cols), np.int32)
        for r, z, c in self.devices:
            ahead = self.place[z // self.subs] - self.place[r]
            table[r, z * CORES + c] = (ahead if c == 0 else -ahead) % self.rows
        return table

    def takers(self):
        return np.array(
            [[[self.along(r, c, -s) for s in range(self.rows)] for c in range(CORES)] for r in range(self.rows)],
            np.int32,
        )


def halves(value):
    high = value.astype(jnp.bfloat16)
    return high, (value - high.astype(jnp.float32)).astype(jnp.bfloat16)


def product(left, right, dims):
    def one(a, b):
        return lax.dot_general(a, b, (dims, ((), ())), preferred_element_type=jnp.float32)

    return one(left[0], right[0]) + (one(left[0], right[1]) + one(left[1], right[0]))


def call(kernel, outs, *args, name, flops=0, smem=0, scratch=()):
    vmem = pl.BlockSpec(memory_space=pltpu.VMEM)
    specs = [pl.BlockSpec(memory_space=pltpu.SMEM)] * smem + [vmem] * (len(args) - smem)
    return pl.pallas_call(
        kernel,
        out_shape=outs,
        in_specs=specs,
        out_specs=[vmem] * len(outs),
        scratch_shapes=list(scratch),
        compiler_params=PARAMS,
        cost_estimate=pl.CostEstimate(flops=flops, bytes_accessed=4 * sum(o.size for o in outs), transcendentals=0),
        name=name,
    )(*args)


def split_kernel(value, high, low):
    high[...], low[...] = halves(value[...])


def split(value):
    return call(split_kernel, [shape(*value.shape, dtype=jnp.bfloat16)] * 2, value, name="split")


class Extra:
    def __init__(self, count, rank, half, width):
        self.count, self.rank, self.half = count, rank, half
        self.folds = 1
        while 2 * self.folds * count * half <= width and rank % (32 * self.folds) == 0:
            self.folds *= 2
        self.height = rank // self.folds

    def lanes(self, fold, index):
        first = (fold * self.count + index) * self.half
        return slice(first, first + self.half)

    def write(self, out, first, index, matrix):
        for f in range(self.folds):
            out[first : first + self.height, self.lanes(f, index)] = matrix[f * self.height : (f + 1) * self.height]

    def read(self, rows, index):
        return jnp.concatenate([rows[:, self.lanes(f, index)] for f in range(self.folds)], axis=0)


def weights_kernel(subs, ahead, behind, where, factor, own, out_ahead, out_behind, turned):
    rank = ahead.rank
    part = factor.shape[0] // (subs * CORES)
    first = where[0] * part
    rows = [factor[pl.ds(pl.multiple_of(first + s * part * CORES, part), part), :] for s in range(subs)]
    turned[...] = jnp.concatenate(rows, axis=0).T

    def columns(steps):
        return turned[pl.ds(pl.multiple_of(where[1 + steps] * rank, rank), rank), :]

    own[...] = columns(0)
    for i in range(ahead.count):
        ahead.write(out_ahead, 0, i, columns(1 + i))
    for i in range(behind.count):
        behind.write(out_behind, 0, i, columns(ahead.count + behind.count - i))


def pack_kernel(subs, cuts, near, far, extra, *outs):
    width = near.shape[1]
    half = near.shape[0]
    part = half // subs
    for n, (a, b, out) in enumerate(zip(cuts, cuts[1:], outs)):
        for s in range(subs):
            out[s * (b - a) : (s + 1) * (b - a), :width] = near[s * part + a : s * part + b, :]
            out[s * (b - a) : (s + 1) * (b - a), width:] = far[s * part + a : s * part + b, :]
        if n == 0:
            height = extra.shape[0] // 2
            out[subs * (b - a) :, :width] = extra[:height, :]
            out[subs * (b - a) :, width:] = extra[height:, :]


def pack(subs, cuts, near, far, extra):
    width = near.shape[1]
    outs = [shape(subs * (b - a) + (extra.shape[0] // 2 if n == 0 else 0), 2 * width) for n, (a, b) in enumerate(zip(cuts, cuts[1:]))]
    return call(functools.partial(pack_kernel, subs, cuts), outs, near, far, extra, name="pack")


def step_kernel(extra, index, has_core, near, far, b0, b1, b2, b3, *refs):
    refs = list(refs)
    half = near.shape[0]
    weights = refs.pop(0)[...] if extra is None else extra.read(far[half:, :], index)
    core_in = [refs.pop(0), refs.pop(0)] if has_core else [None, None]
    gram, *core = refs
    weights = halves(weights)
    total = None
    for rows, high, low, old, new in ((near, b0, b1, core_in[0], core[0]), (far, b2, b3, core_in[1], core[1])):
        pair = halves(rows[:half, :])
        term = product(pair, (high[...], low[...]), ((1,), (1,)))
        total = term if total is None else total + term
        share = product(weights, pair, ((1,), (0,)))
        new[...] = old[...] + share if has_core else share
    gram[...] = total


def step(near, far, block, weights, rank, extra=None, index=None, core=()):
    outs = [shape(near.shape[0], block[0].shape[0])] + [shape(rank, near.shape[1])] * 2
    args = [near, far, *block, *([] if weights is None else [weights]), *core]
    out = call(functools.partial(step_kernel, extra, index, len(core) > 0), outs, *args, name="step", flops=2 * FLOPS)
    return out[0], out[1:]


def piece_kernel(rows, b0, b1, b2, b3, gram):
    count, width = gram.shape[0], b0.shape[1]
    left = product(halves(rows[:count, :width]), (b0[...], b1[...]), ((1,), (1,)))
    gram[...] = left + product(halves(rows[:count, width:]), (b2[...], b3[...]), ((1,), (1,)))


def piece_step(rows, count, block):
    return call(piece_kernel, [shape(count, block[0].shape[0])], rows, *block, name="piece", flops=FLOPS)[0]


def core_kernel(subs, cuts, extra, index, *refs):
    *pieces, old0, old1, new0, new1 = refs
    width = old0.shape[1]
    sizes = [b - a for a, b in zip(cuts, cuts[1:])]
    folded = pieces[0][subs * sizes[0] :, :]
    weights = halves(extra.read(jnp.concatenate([folded[:, :width], folded[:, width:]], axis=0), index))
    for lanes, old, new in ((slice(0, width), old0, new0), (slice(width, None), old1, new1)):
        rows = jnp.concatenate([p[s * n : (s + 1) * n, lanes] for s in range(subs) for p, n in zip(pieces, sizes)], axis=0)
        new[...] = old[...] + product(weights, halves(rows), ((1,), (0,)))


def core_step(subs, cuts, extra, index, pieces, core):
    outs = [shape(*c.shape) for c in core]
    return call(functools.partial(core_kernel, subs, cuts, extra, index), outs, *pieces, *core, name="core", flops=FLOPS // 2)


def finish_kernel(subs, cuts, inverse, counts, where, *refs):
    *refs, share, other_share, gram, core = refs
    kind, sub = where[0], where[1]
    core[...] = share[...] + other_share[...]
    refs = list(refs)
    for steps, count in counts:
        first = 0
        pieces = []
        for _ in range(count):
            for s in range(subs):
                value, received = refs.pop(0), refs.pop(0)
                pieces.append((s, first, value, received))
            first += value.shape[0]

        for s in range(subs):

            @pl.when((kind == steps) & (sub == s))
            def _(chosen=[p for p in pieces if p[0] == s]):
                for _, first, value, received in chosen:
                    gram[first : first + value.shape[0], :] = (value[...] + received[...]) * inverse


class Sums:
    def __init__(self, values, rounds, send):
        self.values, self.rounds, self.send, self.next, self.received = list(values), rounds, send, 0, []

    def advance(self):
        if self.next < len(self.rounds[0]):
            received = [self.send(v, r[self.next]) for v, r in zip(self.values, self.rounds)]
            self.next += 1
            if self.next < len(self.rounds[0]):
                self.values = [v + r for v, r in zip(self.values, received)]
            else:
                self.received = received
        return self

    def finish(self):
        for _ in self.rounds[0]:
            self.advance()

    def held(self):
        return self.received or self.values


def body(tensor, factor):
    layout = Layout(lax.axis_size("row"), lax.axis_size("col"))
    rows, subs = layout.rows, layout.subs
    block, width = tensor.shape
    inverse = 1.0 / (width * layout.cols)
    row, col = lax.axis_index("row"), lax.axis_index("col")
    core = lax.rem(col, CORES)
    part = block // (subs * CORES)
    half = subs * part
    rank = factor.shape[1] // rows

    def send(value, pairs):
        return lax.ppermute(value, AXES, pairs)

    arrived = []

    def fetch(value, steps, *work):
        names = [(arrived, len(arrived) - 2)] if len(arrived) >= 2 else []
        names += [(w.held(), i) for w in work for i in range(subs)]
        if names:
            value, *held = lax.optimization_barrier((value, *(a[i] for a, i in names)))
            for (a, i), h in zip(names, held):
                a[i] = h
        arrived.append(send(value, layout.fetch(steps)))
        return len(arrived) - 1

    def my_rows(value):
        split_rows = value.reshape(subs, CORES, part, value.shape[1])
        return lax.dynamic_index_in_dim(split_rows, core, 1, keepdims=False).reshape(half, value.shape[1])

    classes = {}

    def sums(gram, steps):
        found = Sums(gram.reshape(subs, -1, block), [layout.sums(steps, s) for s in range(subs)], send)
        classes.setdefault(steps, []).append(found)
        return found

    last = rows // 2
    ahead = Extra(last, rank, half, width)
    behind = Extra(rows - 1 - last, rank, half, width)

    near = my_rows(tensor)
    other = send(tensor, layout.swap())
    far = my_rows(other)

    near_row, near = lax.optimization_barrier((row, near))
    table = np.concatenate([np.repeat(layout.takers(), layout.chips, 1).reshape(rows, CORES, layout.chips, rows).swapaxes(1, 2).reshape(rows, layout.cols, rows), layout.classes()[:, :, None]], axis=2)
    found = lax.dynamic_slice(jnp.asarray(table), (near_row, col, 0), (1, 1, rows + 1)).reshape(rows + 1)
    where = jnp.concatenate([core[None].astype(jnp.int32), found])
    place = jnp.stack([found[rows], lax.rem(col // CORES, subs).astype(jnp.int32)])
    own, ride_ahead, ride_behind = call(
        functools.partial(weights_kernel, subs, ahead, behind),
        [shape(rank, half), shape(ahead.height, width), shape(behind.height, width)],
        where,
        factor,
        name="weights",
        smem=1,
        scratch=[pltpu.VMEM((factor.shape[1], half), jnp.float32)],
    )

    first = {1: (near, jnp.concatenate([far, ride_ahead], axis=0), 1), rows - 1: (near, jnp.concatenate([far, ride_behind], axis=0), -1)}
    order = [*range(1, last + 1), *range(rows - 1, last + 1, -1)]
    at = {}

    def got(steps):
        return tuple(arrived[i] for i in at[steps])

    def source(steps):
        if steps in first:
            return first[steps]
        return (*got(steps - 1), 1) if steps <= last else (*got(steps + 1), -1)

    def fetch_half(steps, which, *work):
        value = source(steps)
        at[steps] = (*at.get(steps, ()), fetch(value[which], value[2], *work))

    fetch_half(1, 0)
    fetch_half(1, 1)
    pair = [*split(tensor), *split(other)]
    gram, core_sums = step(near, far, pair, own, rank)
    fresh, older, before = sums(gram, 0), [], 1

    def work_on(steps):
        nonlocal core_sums
        extra, index = (ahead, steps - 1) if steps <= last else (behind, rows - 1 - steps)
        gram, core_sums = step(*got(steps), pair, None, rank, extra, index, core_sums)
        return sums(gram, steps)

    for steps in order[1:]:
        fetch_half(steps, 0, fresh)
        fetch_half(steps, 1)
        older.append(fresh.advance())
        fresh, before = work_on(before), steps

    cuts = [0, part // 2, part * 3 // 4, part]
    near_rows, far_rows, way = source(last + 1)
    p0, p1, p2 = pack(subs, cuts, near_rows, far_rows[:half], far_rows[half:])
    at_pieces = [fetch(p0, way, fresh, *older)]
    older.append(fresh)
    for f in older:
        f.advance()
    at_pieces.append(fetch(p1, way, *older))
    fresh = work_on(before)
    for f in older:
        f.advance()
    at_pieces.append(fetch(p2, way, fresh))
    for f in (*older, fresh):
        f.finish()
    for a, b, i in zip(cuts, cuts[1:], at_pieces):
        sums(piece_step(arrived[i], subs * (b - a), pair), last + 1).finish()

    share, other_share = core_step(subs, cuts, behind, behind.count - 1, [arrived[i] for i in at_pieces], core_sums)
    counts = [(steps, len(found)) for steps, found in classes.items()]
    sent = [x for found in classes.values() for f in found for pair in zip(f.values, f.received) for x in pair]
    return tuple(
        call(
            functools.partial(finish_kernel, subs, cuts, inverse, counts),
            [shape(part, block), shape(rank, width)],
            place,
            *sent,
            share,
            send(other_share, layout.swap()),
            name="finish",
            smem=1,
        )
    )


def solution(mesh):
    placed = (P("row", "col"), P("row", None))
    return jax.shard_map(
        body,
        mesh=mesh,
        in_specs=placed,
        out_specs=(P("col", "row"), P("row", "col")),
        check_vma=False,
    )
```

```python
import functools

import jax
import jax.numpy as jnp
import numpy as np
from jax import lax
from jax.experimental import pallas as pl
from jax.experimental.pallas import tpu as pltpu
from jax.sharding import PartitionSpec as P

AXES = ("row", "col")
CORES = 2
CUTS = (0, 1, 2, 4, 6, 8)
BACK = (4, 4, 6)
PARAMS = pltpu.CompilerParams(vmem_limit_bytes=40 * 2**20)


def shape(*dims, dtype=jnp.float32):
    return jax.ShapeDtypeStruct(dims, dtype)


class Layout:
    def __init__(self, rows, cols):
        self.rows, self.cols, self.chips = rows, cols, cols // CORES
        self.subs = self.chips // rows
        self.rounds = self.chips.bit_length() - 1
        assert rows % 2 == 0 and rows >= 4 and self.chips == 1 << self.rounds and self.subs * rows == self.chips
        self.ring = [*range(0, rows, 2), *reversed(range(1, rows, 2))]
        self.place = {r: i for i, r in enumerate(self.ring)}
        self.devices = [(r, z, c) for r in range(rows) for z in range(self.chips) for c in range(CORES)]

    def flat(self, r, z, c):
        return r * self.cols + z * CORES + c

    def along(self, r, c, steps):
        return self.ring[(self.place[r] + (steps if c == 0 else -steps)) % self.rows]

    def swap(self):
        return [(self.flat(r, z, c), self.flat(r, z, 1 - c)) for r, z, c in self.devices]

    def fetch(self, steps):
        return [(self.flat(self.along(r, c, steps), z, c), self.flat(r, z, c)) for r, z, c in self.devices]

    def exchange(self, bit):
        return [(self.flat(r, z, c), self.flat(r, z ^ (1 << bit), c)) for r, z, c in self.devices]

    def slot(self, target, z):
        return int(format(target ^ z, f"0{self.rounds}b")[::-1], 2)

    def table(self):
        table = np.zeros((self.rows, self.cols, 1 + self.rows + self.chips), np.int32)
        for r, z, c in self.devices:
            takers = [self.along(r, c, -s) for s in range(self.rows)]
            slots = [self.slot(self.along(r, c, s) * self.subs + p, z) for s in range(self.rows) for p in range(self.subs)]
            table[r, z * CORES + c] = [c, *takers, *slots]
        return table


def halves(value):
    high = value.astype(jnp.bfloat16)
    return high, (value - high.astype(jnp.float32)).astype(jnp.bfloat16)


def product(left, right, dims):
    def one(a, b):
        return lax.dot_general(a, b, (dims, ((), ())), preferred_element_type=jnp.float32)

    return one(left[0], right[0]) + (one(left[0], right[1]) + one(left[1], right[0]))


def call(kernel, outs, *args, name, flops=0, smem=0, scratch=()):
    vmem = pl.BlockSpec(memory_space=pltpu.VMEM)
    specs = [pl.BlockSpec(memory_space=pltpu.SMEM)] * smem + [vmem] * (len(args) - smem)
    return pl.pallas_call(
        kernel,
        out_shape=outs,
        in_specs=specs,
        out_specs=[vmem] * len(outs),
        scratch_shapes=list(scratch),
        compiler_params=PARAMS,
        cost_estimate=pl.CostEstimate(flops=flops, bytes_accessed=4 * sum(o.size for o in outs), transcendentals=0),
        name=name,
    )(*args)


def call(kernel, outs, *args, name, flops=0, smem=0, scratch=()):
    vmem = pl.BlockSpec(memory_space=pltpu.VMEM)
    specs = [pl.BlockSpec(memory_space=pltpu.SMEM)] * smem + [vmem] * (len(args) - smem)
    return pl.pallas_call(
        kernel,
        out_shape=outs,
        in_specs=specs,
        out_specs=[vmem] * len(outs),
        scratch_shapes=list(scratch),
        compiler_params=PARAMS,
        cost_estimate=pl.CostEstimate(flops=flops, bytes_accessed=4 * sum(o.size for o in outs), transcendentals=0),
        name=name,
    )(*args)


class Extra:
    def __init__(self, count, rank, half, width):
        self.count, self.rank, self.half, self.width = count, rank, half, width
        self.folds = 1
        while 2 * self.folds * count * half <= width and rank % (16 * self.folds) == 0:
            self.folds *= 2
        self.height = rank // self.folds

    def lanes(self, fold, index):
        first = (fold * self.count + index) * self.half
        return slice(first, first + self.half)

    def write(self, out, index, matrix):
        for f in range(self.folds):
            out[:, self.lanes(f, index)] = matrix[f * self.height : (f + 1) * self.height]

    def read(self, rows, index):
        return jnp.concatenate([rows[:, self.lanes(f, index)] for f in range(self.folds)], axis=0)


def weights_kernel(subs, ahead, behind, where, factor, own, out_ahead, out_behind, turned):
    rank = ahead.rank
    part = factor.shape[0] // (subs * CORES)
    size = part // 2
    for n in range(CORES):
        core = (where[0] + n) % CORES
        rows = [
            factor[pl.ds(pl.multiple_of((s * CORES + core) * part + g * size, size), size), :]
            for g in range(2)
            for s in range(subs)
        ]
        turned[n] = jnp.concatenate(rows, axis=0).T

    def columns(steps, n=0):
        return turned[n, pl.ds(pl.multiple_of(where[1 + steps] * rank, rank), rank), :]

    for n in range(CORES):
        own[n] = columns(0, n)
    for i in range(ahead.count):
        ahead.write(out_ahead, i, columns(1 + i))
    for i in range(behind.count):
        behind.write(out_behind, i, columns(ahead.count + behind.count - i))


def prepare_kernel(subs, cuts, tensor, ride_ahead, ride_behind, high, low, *outs):
    high[...], low[...] = halves(tensor[...])
    part = tensor.shape[0] // (subs * CORES)
    for a, b, out in zip([cuts[0], *cuts], [cuts[1], *cuts[1:]], outs):
        size = b - a
        for c in range(CORES):
            for s in range(subs):
                first, to = (s * CORES + c) * part + a, (c * subs + s) * size
                out[to : to + size, :] = tensor[first : first + size, :]
    rows = CORES * subs * (cuts[1] - cuts[0])
    outs[0][rows:, :] = ride_ahead[...]
    outs[1][rows:, :] = ride_behind[...]


def gram_kernel(subs, where, *refs):
    *chunks, high, low, keep, send = refs
    size = keep.shape[1]
    rows = CORES * subs * size
    left = halves(jnp.concatenate([c[:rows, :] for c in chunks], axis=0))
    total = product(left, (high[...], low[...]), ((1,), (1,)))
    for k in range(len(chunks)):
        for c in range(CORES):
            for s in range(subs):
                slot = where[1 + len(chunks) + k * subs + s]
                first = ((k * CORES + c) * subs + s) * size

                @pl.when(where[0] == c)
                def _(slot=slot, first=first):
                    keep[slot] = total[first : first + size]

                @pl.when(where[0] != c)
                def _(slot=slot, first=first):
                    send[slot] = total[first : first + size]


def fold_kernel(keep, received, new_keep, new_send):
    slots = new_keep.shape[0]
    new_keep[...] = keep[:slots] + received[:slots]
    new_send[...] = keep[slots:] + received[slots:]


def core_kernel(subs, group, sizes, extras, where, *refs):
    *refs, out = refs
    refs = list(refs)
    own = refs.pop(0)
    mine = [refs.pop(0) for _ in extras]
    other = refs.pop(0)
    half = own.shape[2] // 2
    lanes = slice(group * half, (group + 1) * half)
    weights = [(own[0][:, lanes], own[1][:, lanes])]
    for rows, (extra, index, (extra2, index2, first)) in zip(mine, extras):
        near = extra.read(rows[rows.shape[0] - extra.height :, :], index)
        far = extra2.read(other[first : first + extra2.height, :], index2)
        weights.append((near[:, lanes], far[:, lanes]))
    first = where[0] == 0
    sides = [jnp.where(first, w[n], w[1 - n]) for w in weights for n in range(CORES)]
    weights = halves(jnp.concatenate(sides, axis=1))
    count = len(sizes)
    whole = []
    for k in range(len(extras) + 1):
        chunks = refs[k * count : (k + 1) * count]
        for c in range(CORES):
            for s in range(subs):
                for chunk, size in zip(chunks, sizes):
                    at = (c * subs + s) * size
                    whole.append(chunk[at : at + size, :])
    share = product(weights, halves(jnp.concatenate(whole, axis=0)), ((1,), (0,)))
    before = refs[(len(extras) + 1) * count :]
    out[...] = before[0][...] + share if before else share


def finish_kernel(cuts, inverse, *refs):
    *refs, gram = refs
    for n, (a, b) in enumerate(zip(cuts, cuts[1:])):
        gram[a:b, :] = (refs[2 * n][0] + refs[2 * n + 1][0]) * inverse


def body(tensor, factor):
    layout = Layout(lax.axis_size("row"), lax.axis_size("col"))
    rows, subs, chips = layout.rows, layout.subs, layout.chips
    block, width = tensor.shape
    inverse = 1.0 / (width * layout.cols)
    row, col = lax.axis_index("row"), lax.axis_index("col")
    core = lax.rem(col, CORES)
    part = block // (subs * CORES)
    rank = factor.shape[1] // rows
    cuts = [part * n // 8 for n in CUTS]
    sizes = [b - a for a, b in zip(cuts, cuts[1:])]
    chunks = range(len(sizes))
    bf16 = jnp.bfloat16

    def send(value, pairs):
        return lax.ppermute(value, AXES, pairs)

    arrived = []

    def fetch(value, steps, work=(), back=BACK[0]):
        names = [(arrived, len(arrived) - back)] if len(arrived) >= back else []
        names += work
        if names:
            value, *held = lax.optimization_barrier((value, *(a[i] for a, i in names)))
            for (a, i), h in zip(names, held):
                a[i] = h
        arrived.append(send(value, layout.fetch(steps)))
        return len(arrived) - 1

    size = sizes[0]
    split_rows = tensor.reshape(subs, CORES, part, width).swapaxes(0, 1)
    own = {(0, w): split_rows[:, :, :size].reshape(CORES * subs * size, width) for w in (1, -1)}
    at = {(0, s): fetch(own[0, w], w) for s, w in ((1, 1), (rows - 1, -1))}

    table = jnp.asarray(layout.table())
    where = lax.dynamic_slice(table, (row, col, 0), (1, 1, table.shape[2])).reshape(-1)
    half = subs * part
    last = rows // 2
    ahead, behind = Extra(last, rank, half, width), Extra(rows - 1 - last, rank, half, width)
    own_weights, ride_ahead, ride_behind = call(
        functools.partial(weights_kernel, subs, ahead, behind),
        [shape(CORES, rank, half), shape(ahead.height, width), shape(behind.height, width)],
        where,
        factor,
        name="weights",
        smem=1,
        scratch=[pltpu.VMEM((CORES, factor.shape[1], half), jnp.float32)],
    )
    heights = [CORES * subs * n for n in (sizes[1], *sizes[1:])]
    heights[0] += ahead.height
    heights[1] += behind.height
    ready = call(
        functools.partial(prepare_kernel, subs, cuts[1:]),
        [shape(block, width, dtype=bf16)] * 2 + [shape(n, width) for n in heights],
        tensor,
        ride_ahead,
        ride_behind,
        name="prepare",
    )
    pair = list(ready[:2])
    own.update({(n, w): p for n, p in enumerate(ready[4:], 2) for w in (1, -1)})
    own[1, 1], own[1, -1] = ready[2:4]

    order = [1, *(s for i in range(1, last) for s in (rows - i, i + 1))]

    def got(chunk, steps, way=1):
        return own[chunk, way] if steps == 0 else arrived[at[chunk, steps]]

    def gather(chunk, steps, work, back):
        way = 1 if steps <= last else -1
        value = got(chunk, steps - 1 if steps <= last else (steps + 1) % rows, way)
        at[chunk, steps] = fetch(value, way, work, back)

    def grams(chunk):
        size = sizes[chunk]
        return call(
            functools.partial(gram_kernel, subs),
            [shape(chips, size, block)] * 2,
            where,
            *(got(chunk, s) for s in range(rows)),
            *pair,
            name="gram",
            flops=12 * rows * subs * size * block * width,
            smem=1,
        )

    exchanges = [layout.swap(), *(layout.exchange(bit) for bit in range(layout.rounds))]

    def fold(state, n):
        keep, out = state
        received = send(out, exchanges[n])
        if n + 1 == len(exchanges):
            return [keep, received]
        return call(fold_kernel, [shape(keep.shape[0] // 2, *keep.shape[1:])] * 2, keep, received, name="fold")

    ride = [(ahead, s - 1) if s <= last else (behind, rows - 1 - s) for s in range(1, rows)]

    def swap_weights():
        held = [got(1, s) for s in range(1, rows)]
        return send(jnp.concatenate([v[v.shape[0] - e.height :] for v, (e, _) in zip(held, ride)], axis=0), layout.swap())

    def core_share(group, shares):
        parts = [n for n in chunks if cuts[n] * 2 // part == group]
        firsts = np.cumsum([0, *(e.height for e, _ in ride)])
        extras = [(*ride[s - 1], (*ride[rows - s - 1], int(firsts[rows - s - 1]))) for s in range(1, rows)]
        return call(
            functools.partial(core_kernel, subs, group, [sizes[n] for n in parts], extras),
            [shape(rank, width)],
            where,
            own_weights,
            *(got(1, s) for s in range(1, rows)),
            other_weights,
            *(got(n, s) for s in range(rows) for n in parts),
            *shares,
            name="core",
            flops=6 * rank * half * rows * width,
            smem=1,
        )

    states, rounds = {}, {}

    def advance(n):
        if n in states and rounds[n] < len(exchanges):
            states[n] = list(fold(states[n], rounds[n]))
            rounds[n] += 1

    def held(n):
        return [(states[n], 0), (states[n], 1)] if n in states else []

    def plan():
        for n in chunks:
            for i, steps in enumerate(order):
                if i == len(order) - 1 and n + 1 < len(sizes):
                    yield n + 1, 0, order[0]
                if i > 0 or n == 0:
                    yield n, i, steps

    for n, i, steps in plan():
        final = i == len(order) - 1
        if (n, steps) not in at:
            gather(n, steps, [(pair, 0)] if n == 0 else [], BACK[2] if final else BACK[min(i, 1)])
        if not final:
            continue
        for back, count in ((1, 2), (2, len(exchanges))):
            while n - back in rounds and rounds[n - back] < count:
                advance(n - back)
        names = [t for back in (1, 2, 3) for t in held(n - back)]
        if names:
            own[n, 1], *values = lax.optimization_barrier((own[n, 1], *(a[i] for a, i in names)))
            for (a, i), value in zip(names, values):
                a[i] = value
        states[n], rounds[n] = list(grams(n)), 0
    other_weights = swap_weights()
    share = core_share(0, [])
    while any(rounds[i] < len(exchanges) for i in chunks):
        for i in chunks:
            if i == n and rounds[n] == 2:
                states[n][0], states[n - 1][1] = lax.optimization_barrier((states[n][0], states[n - 1][1]))
            advance(i)
        if rounds[n] == 2:
            own_weights, states[n][0] = lax.optimization_barrier((own_weights, states[n][0]))
    done = [a for n in chunks for a in states[n]]

    (core_rows,) = core_share(1, share)
    (gram,) = call(functools.partial(finish_kernel, cuts, inverse), [shape(part, block)], *done, name="finish")
    return (gram, core_rows)


def solution(mesh):
    placed = (P("row", "col"), P("row", None))
    return jax.shard_map(
        body,
        mesh=mesh,
        in_specs=placed,
        out_specs=(P("col", "row"), P("row", "col")),
        check_vma=False,
    )
```

```python
import functools

import jax
import jax.numpy as jnp
import numpy as np
from jax import lax
from jax.experimental import pallas as pl
from jax.experimental.pallas import tpu as pltpu
from jax.sharding import PartitionSpec as P

AXES = ("row", "col")
CORES = 2
HINT = 10
CUTS = (0, 1, 2, 4, 6, 8)
BACK = (4, 4, 6)
PARAMS = pltpu.CompilerParams(vmem_limit_bytes=40 * 2**20)


def shape(*dims, dtype=jnp.float32):
    return jax.ShapeDtypeStruct(dims, dtype)


class Layout:
    def __init__(self, rows, cols):
        self.rows, self.cols, self.chips = rows, cols, cols // CORES
        self.subs = self.chips // rows
        self.rounds = self.chips.bit_length() - 1
        assert rows % 2 == 0 and rows >= 4 and self.chips == 1 << self.rounds and self.subs * rows == self.chips
        self.ring = [*range(0, rows, 2), *reversed(range(1, rows, 2))]
        self.place = {r: i for i, r in enumerate(self.ring)}
        self.devices = [(r, z, c) for r in range(rows) for z in range(self.chips) for c in range(CORES)]

    def flat(self, r, z, c):
        return r * self.cols + z * CORES + c

    def along(self, r, c, steps):
        return self.ring[(self.place[r] + (steps if c == 0 else -steps)) % self.rows]

    def swap(self):
        return [(self.flat(r, z, c), self.flat(r, z, 1 - c)) for r, z, c in self.devices]

    def fetch(self, steps):
        return [(self.flat(self.along(r, c, steps), z, c), self.flat(r, z, c)) for r, z, c in self.devices]

    def exchange(self, bit):
        return [(self.flat(r, z, c), self.flat(r, z ^ (1 << bit), c)) for r, z, c in self.devices]

    def slot(self, target, z):
        return int(format(target ^ z, f"0{self.rounds}b")[::-1], 2)

    def table(self):
        table = np.zeros((self.rows, self.cols, 1 + self.rows + self.chips), np.int32)
        for r, z, c in self.devices:
            takers = [self.along(r, c, -s) for s in range(self.rows)]
            slots = [self.slot(self.along(r, c, s) * self.subs + p, z) for s in range(self.rows) for p in range(self.subs)]
            table[r, z * CORES + c] = [c, *takers, *slots]
        return table


def halves(value):
    high = value.astype(jnp.bfloat16)
    return high, (value - high.astype(jnp.float32)).astype(jnp.bfloat16)


def product(left, right, dims):
    def one(a, b):
        return lax.dot_general(a, b, (dims, ((), ())), preferred_element_type=jnp.float32)

    return one(left[0], right[0]) + (one(left[0], right[1]) + one(left[1], right[0]))


def call(kernel, outs, *args, name, flops=0, smem=0, scratch=()):
    vmem = pl.BlockSpec(memory_space=pltpu.VMEM)
    specs = [pl.BlockSpec(memory_space=pltpu.SMEM)] * smem + [vmem] * (len(args) - smem)
    return pl.pallas_call(
        kernel,
        out_shape=outs,
        in_specs=specs,
        out_specs=[vmem] * len(outs),
        scratch_shapes=list(scratch),
        compiler_params=PARAMS,
        cost_estimate=pl.CostEstimate(flops=flops // HINT, bytes_accessed=4 * sum(o.size for o in outs) // HINT, transcendentals=0),
        name=name,
    )(*args)


def call(kernel, outs, *args, name, flops=0, smem=0, scratch=()):
    vmem = pl.BlockSpec(memory_space=pltpu.VMEM)
    specs = [pl.BlockSpec(memory_space=pltpu.SMEM)] * smem + [vmem] * (len(args) - smem)
    return pl.pallas_call(
        kernel,
        out_shape=outs,
        in_specs=specs,
        out_specs=[vmem] * len(outs),
        scratch_shapes=list(scratch),
        compiler_params=PARAMS,
        cost_estimate=pl.CostEstimate(flops=flops // HINT, bytes_accessed=4 * sum(o.size for o in outs) // HINT, transcendentals=0),
        name=name,
    )(*args)


class Extra:
    def __init__(self, count, rank, half, width):
        self.count, self.rank, self.half, self.width = count, rank, half, width
        self.folds = 1
        while 2 * self.folds * count * half <= width and rank % (16 * self.folds) == 0:
            self.folds *= 2
        self.height = rank // self.folds

    def lanes(self, fold, index):
        first = (fold * self.count + index) * self.half
        return slice(first, first + self.half)

    def write(self, out, index, matrix):
        for f in range(self.folds):
            out[:, self.lanes(f, index)] = matrix[f * self.height : (f + 1) * self.height]

    def read(self, rows, index):
        return jnp.concatenate([rows[:, self.lanes(f, index)] for f in range(self.folds)], axis=0)


def weights_kernel(subs, ahead, behind, where, factor, own, out_ahead, out_behind, turned):
    rank = ahead.rank
    part = factor.shape[0] // (subs * CORES)
    size = part // 2
    for n in range(CORES):
        core = (where[0] + n) % CORES
        rows = [
            factor[pl.ds(pl.multiple_of((s * CORES + core) * part + g * size, size), size), :]
            for g in range(2)
            for s in range(subs)
        ]
        turned[n] = jnp.concatenate(rows, axis=0).T

    def columns(steps, n=0):
        return turned[n, pl.ds(pl.multiple_of(where[1 + steps] * rank, rank), rank), :]

    for n in range(CORES):
        own[n] = columns(0, n)
    for i in range(ahead.count):
        ahead.write(out_ahead, i, columns(1 + i))
    for i in range(behind.count):
        behind.write(out_behind, i, columns(ahead.count + behind.count - i))


def prepare_kernel(subs, cuts, tensor, ride_ahead, ride_behind, high, low, *outs):
    high[...], low[...] = halves(tensor[...])
    part = tensor.shape[0] // (subs * CORES)
    for a, b, out in zip([cuts[0], *cuts], [cuts[1], *cuts[1:]], outs):
        size = b - a
        for c in range(CORES):
            for s in range(subs):
                first, to = (s * CORES + c) * part + a, (c * subs + s) * size
                out[to : to + size, :] = tensor[first : first + size, :]
    rows = CORES * subs * (cuts[1] - cuts[0])
    outs[0][rows:, :] = ride_ahead[...]
    outs[1][rows:, :] = ride_behind[...]


def gram_kernel(subs, where, *refs):
    *chunks, high, low, keep, send = refs
    size = keep.shape[1]
    rows = CORES * subs * size
    left = halves(jnp.concatenate([c[:rows, :] for c in chunks], axis=0))
    total = product(left, (high[...], low[...]), ((1,), (1,)))
    for k in range(len(chunks)):
        for c in range(CORES):
            for s in range(subs):
                slot = where[1 + len(chunks) + k * subs + s]
                first = ((k * CORES + c) * subs + s) * size

                @pl.when(where[0] == c)
                def _(slot=slot, first=first):
                    keep[slot] = total[first : first + size]

                @pl.when(where[0] != c)
                def _(slot=slot, first=first):
                    send[slot] = total[first : first + size]


def fold_kernel(keep, received, new_keep, new_send):
    slots = new_keep.shape[0]
    new_keep[...] = keep[:slots] + received[:slots]
    new_send[...] = keep[slots:] + received[slots:]


def core_kernel(subs, group, sizes, extras, where, *refs):
    *refs, out = refs
    refs = list(refs)
    own = refs.pop(0)
    mine = [refs.pop(0) for _ in extras]
    other = refs.pop(0)
    half = own.shape[2] // 2
    lanes = slice(group * half, (group + 1) * half)
    weights = [(own[0][:, lanes], own[1][:, lanes])]
    for rows, (extra, index, (extra2, index2, first)) in zip(mine, extras):
        near = extra.read(rows[rows.shape[0] - extra.height :, :], index)
        far = extra2.read(other[first : first + extra2.height, :], index2)
        weights.append((near[:, lanes], far[:, lanes]))
    first = where[0] == 0
    sides = [jnp.where(first, w[n], w[1 - n]) for w in weights for n in range(CORES)]
    weights = halves(jnp.concatenate(sides, axis=1))
    count = len(sizes)
    whole = []
    for k in range(len(extras) + 1):
        chunks = refs[k * count : (k + 1) * count]
        for c in range(CORES):
            for s in range(subs):
                for chunk, size in zip(chunks, sizes):
                    at = (c * subs + s) * size
                    whole.append(chunk[at : at + size, :])
    share = product(weights, halves(jnp.concatenate(whole, axis=0)), ((1,), (0,)))
    before = refs[(len(extras) + 1) * count :]
    out[...] = before[0][...] + share if before else share


def finish_kernel(cuts, inverse, *refs):
    *refs, gram = refs
    for n, (a, b) in enumerate(zip(cuts, cuts[1:])):
        gram[a:b, :] = (refs[2 * n][0] + refs[2 * n + 1][0]) * inverse


def body(tensor, factor):
    layout = Layout(lax.axis_size("row"), lax.axis_size("col"))
    rows, subs, chips = layout.rows, layout.subs, layout.chips
    block, width = tensor.shape
    inverse = 1.0 / (width * layout.cols)
    row, col = lax.axis_index("row"), lax.axis_index("col")
    core = lax.rem(col, CORES)
    part = block // (subs * CORES)
    rank = factor.shape[1] // rows
    cuts = [part * n // 8 for n in CUTS]
    sizes = [b - a for a, b in zip(cuts, cuts[1:])]
    chunks = range(len(sizes))
    bf16 = jnp.bfloat16

    def send(value, pairs):
        return lax.ppermute(value, AXES, pairs)

    arrived = []

    def fetch(value, steps, work=(), back=BACK[0]):
        names = [(arrived, len(arrived) - back)] if len(arrived) >= back else []
        names += work
        if names:
            value, *held = lax.optimization_barrier((value, *(a[i] for a, i in names)))
            for (a, i), h in zip(names, held):
                a[i] = h
        arrived.append(send(value, layout.fetch(steps)))
        return len(arrived) - 1

    size = sizes[0]
    split_rows = tensor.reshape(subs, CORES, part, width).swapaxes(0, 1)
    own = {(0, w): split_rows[:, :, :size].reshape(CORES * subs * size, width) for w in (1, -1)}
    at = {(0, s): fetch(own[0, w], w) for s, w in ((1, 1), (rows - 1, -1))}

    table = jnp.asarray(layout.table())
    where = lax.dynamic_slice(table, (row, col, 0), (1, 1, table.shape[2])).reshape(-1)
    half = subs * part
    last = rows // 2
    ahead, behind = Extra(last, rank, half, width), Extra(rows - 1 - last, rank, half, width)
    own_weights, ride_ahead, ride_behind = call(
        functools.partial(weights_kernel, subs, ahead, behind),
        [shape(CORES, rank, half), shape(ahead.height, width), shape(behind.height, width)],
        where,
        factor,
        name="weights",
        smem=1,
        scratch=[pltpu.VMEM((CORES, factor.shape[1], half), jnp.float32)],
    )
    heights = [CORES * subs * n for n in (sizes[1], *sizes[1:])]
    heights[0] += ahead.height
    heights[1] += behind.height
    ready = call(
        functools.partial(prepare_kernel, subs, cuts[1:]),
        [shape(block, width, dtype=bf16)] * 2 + [shape(n, width) for n in heights],
        tensor,
        ride_ahead,
        ride_behind,
        name="prepare",
    )
    pair = list(ready[:2])
    own.update({(n, w): p for n, p in enumerate(ready[4:], 2) for w in (1, -1)})
    own[1, 1], own[1, -1] = ready[2:4]

    order = [1, *(s for i in range(1, last) for s in (rows - i, i + 1))]

    def got(chunk, steps, way=1):
        return own[chunk, way] if steps == 0 else arrived[at[chunk, steps]]

    def gather(chunk, steps, work, back):
        way = 1 if steps <= last else -1
        value = got(chunk, steps - 1 if steps <= last else (steps + 1) % rows, way)
        at[chunk, steps] = fetch(value, way, work, back)

    def grams(chunk):
        size = sizes[chunk]
        return call(
            functools.partial(gram_kernel, subs),
            [shape(chips, size, block)] * 2,
            where,
            *(got(chunk, s) for s in range(rows)),
            *pair,
            name="gram",
            flops=12 * rows * subs * size * block * width,
            smem=1,
        )

    exchanges = [layout.swap(), *(layout.exchange(bit) for bit in range(layout.rounds))]

    def fold(state, n):
        keep, out = state
        received = send(out, exchanges[n])
        if n + 1 == len(exchanges):
            return [keep, received]
        return call(fold_kernel, [shape(keep.shape[0] // 2, *keep.shape[1:])] * 2, keep, received, name="fold")

    ride = [(ahead, s - 1) if s <= last else (behind, rows - 1 - s) for s in range(1, rows)]

    def swap_weights():
        held = [got(1, s) for s in range(1, rows)]
        return send(jnp.concatenate([v[v.shape[0] - e.height :] for v, (e, _) in zip(held, ride)], axis=0), layout.swap())

    def core_share(group, shares):
        parts = [n for n in chunks if cuts[n] * 2 // part == group]
        firsts = np.cumsum([0, *(e.height for e, _ in ride)])
        extras = [(*ride[s - 1], (*ride[rows - s - 1], int(firsts[rows - s - 1]))) for s in range(1, rows)]
        return call(
            functools.partial(core_kernel, subs, group, [sizes[n] for n in parts], extras),
            [shape(rank, width)],
            where,
            own_weights,
            *(got(1, s) for s in range(1, rows)),
            other_weights,
            *(got(n, s) for s in range(rows) for n in parts),
            *shares,
            name="core",
            flops=6 * rank * half * rows * width,
            smem=1,
        )

    states, rounds = {}, {}

    def advance(n):
        if n in states and rounds[n] < len(exchanges):
            states[n] = list(fold(states[n], rounds[n]))
            rounds[n] += 1

    def held(n):
        return [(states[n], 0), (states[n], 1)] if n in states else []

    def plan():
        for n in chunks:
            for i, steps in enumerate(order):
                if i == len(order) - 1 and n + 1 < len(sizes):
                    yield n + 1, 0, order[0]
                if i > 0 or n == 0:
                    yield n, i, steps

    for n, i, steps in plan():
        final = i == len(order) - 1
        if (n, steps) not in at:
            gather(n, steps, [(pair, 0)] if n == 0 else [], BACK[2] if final else BACK[min(i, 1)])
        if not final:
            continue
        for back, count in ((1, 2), (2, len(exchanges))):
            while n - back in rounds and rounds[n - back] < count:
                advance(n - back)
        names = [t for back in (1, 2, 3) for t in held(n - back)]
        if names:
            own[n, 1], *values = lax.optimization_barrier((own[n, 1], *(a[i] for a, i in names)))
            for (a, i), value in zip(names, values):
                a[i] = value
        states[n], rounds[n] = list(grams(n)), 0
    other_weights = swap_weights()
    share = core_share(0, [])
    while any(rounds[i] < len(exchanges) for i in chunks):
        for i in chunks:
            if i == n and rounds[n] == 2:
                states[n][0], states[n - 1][1] = lax.optimization_barrier((states[n][0], states[n - 1][1]))
            advance(i)
        if rounds[n] == 2:
            own_weights, states[n][0] = lax.optimization_barrier((own_weights, states[n][0]))
    done = [a for n in chunks for a in states[n]]

    (core_rows,) = core_share(1, share)
    (gram,) = call(functools.partial(finish_kernel, cuts, inverse), [shape(part, block)], *done, name="finish")
    return (gram, core_rows)


def solution(mesh):
    placed = (P("row", "col"), P("row", None))
    return jax.shard_map(
        body,
        mesh=mesh,
        in_specs=placed,
        out_specs=(P("col", "row"), P("row", "col")),
        check_vma=False,
    )
```
